1024 devices in a mesh: dp: 32 (over z, x_hi), mp: 32 (over y, x_lo, core).
Axes of the slice: x: 8 (x_hi: 4, x_lo: 2; x = x_hi * 2 + x_lo), y: 8, z: 8, core: 2. Of those that a mesh axis runs over, the one named last changes fastest.
Arguments:
- tokens: bfloat16 [8192, 3072], P('dp', 'mp'), may hold values from -6 to 6
- w_in: bfloat16 [3072, 12288], P(None, 'mp'), may hold values from -0.21875 to 0.21875
- hidden_grad: bfloat16 [8192, 12288], P('dp', 'mp'), may hold values from -6 to 6
Outputs:
- input_grad: bfloat16 [8192, 3072], P('dp', 'mp')
- weight_grad: bfloat16 [3072, 12288], P('dp', 'mp')
The draws below stay inside these ranges and needn't reach their ends.
All inputs are finite; a program needn't handle non-finite values.
Results may differ from the reference program's by a relative error of at most 0.0049.
Values may be sent and summed in bfloat16 or wider, within the bound.
No kernel may reach another device: no remote copies, remote signals or barrier semaphores. Data moves between devices by JAX's collectives and lax.ppermute only.
A program may use at most 64 MiB of HBM per device.

```python
import jax
import jax.numpy as jnp

D = 3072
FF = 12288
TOKENS = 8192


def with_spikes(entries, rng, source, target, parts, factor):
    def block_of(axis_at):
        return (jnp.arange(entries.shape[axis_at]) // (entries.shape[axis_at] // parts)).reshape((-1,) + (1,) * (entries.ndim - 1 - axis_at))

    first = jax.random.permutation(rng, parts)[block_of(target)]
    second = (block_of(target) + parts // 2) % parts
    return jnp.where((block_of(source) == first) | (block_of(source) == second), factor * entries, entries)


def shard_levels(stream_key, dims, pieces, smallest, high):
    gain = 1.0
    for position, shards_of in pieces:
        heights = jax.random.uniform(jax.random.fold_in(jax.random.fold_in(stream_key, 6), position), (shards_of,), jnp.float32, smallest / len(pieces), high / len(pieces))
        gain = gain * jnp.repeat(jnp.exp(heights), dims[position] // shards_of).reshape((-1,) + (1,) * (len(dims) - 1 - position))
    return gain


def normal_values(own_key, dims, spread, bound, split=(), dtype=jnp.bfloat16):
    array = spread * jax.random.normal(own_key, dims, jnp.float32)
    if split:
        array = array * shard_levels(own_key, dims, split, -0.22, 0.18)
    return jnp.clip(array, -bound, bound).astype(dtype)


def heavy_noise(key, dims, scale, limit, pieces, heavy, dtype=jnp.bfloat16):
    entries = scale * jax.random.normal(key, dims, jnp.float32)
    if pieces:
        entries = entries * shard_levels(key, dims, pieces, -0.22, 0.18)
    return jnp.clip(with_spikes(entries, jax.random.fold_in(key, 3), *heavy), -limit, limit).astype(dtype)


def setup_inputs(seed: int = 0) -> dict:
    key_list = jax.random.split(jax.random.key(seed), 4)
    return {
        "tokens": heavy_noise(key_list[0], (TOKENS, D), 1.0, 6.0, ((0, 32), (1, 32)), (0, 1, 32, 2.75)),
        "w_in": heavy_noise(key_list[1], (D, FF), D ** -0.5, 0.21875, ((1, 32),), (1, 0, 32, 2.75)),
        "hidden_grad": normal_values(key_list[2], (TOKENS, FF), 1.0, 6.0, ((0, 32), (1, 32))),
    }


def gelu_slope(pre):
    coef = 0.7978845608028654
    inner = coef * (pre + 0.044715 * pre * pre * pre)
    tval = jnp.tanh(inner)
    return 0.5 * (1.0 + tval) + 0.5 * pre * (1.0 - tval * tval) * coef * (1.0 + 3.0 * 0.044715 * pre * pre)


def reference(tokens, w_in, hidden_grad):
    pre = jnp.dot(tokens, w_in, preferred_element_type=jnp.float32)
    pre_grad = (hidden_grad.astype(jnp.float32) * gelu_slope(pre)).astype(jnp.bfloat16)
    input_sum = jnp.dot(pre_grad, w_in.T, preferred_element_type=jnp.float32)
    weight_sum = jnp.dot(tokens.T, pre_grad, preferred_element_type=jnp.float32)
    return input_sum.astype(jnp.bfloat16), weight_sum.astype(jnp.bfloat16)
```

```python
import jax
import jax.numpy as jnp
from jax import lax
from jax.experimental import pallas as pl
from jax.experimental.pallas import tpu as pltpu
from jax.sharding import Mesh, PartitionSpec as P

DP = ("z", "xh")
MP = ("y", "xl", "c")
F32 = jnp.float32
BF16 = jnp.bfloat16
VMEM = pl.BlockSpec(memory_space=pltpu.VMEM)
SMEM = pl.BlockSpec(memory_space=pltpu.SMEM)


def gelu_slope(pre):
    coef = 0.7978845608028654
    inner = coef * (pre + 0.044715 * pre * pre * pre)
    tval = jnp.tanh(inner)
    return 0.5 * (1.0 + tval) + 0.5 * pre * (1.0 - tval * tval) * coef * (
        1.0 + 3.0 * 0.044715 * pre * pre
    )


def hidden_kernel(core_ref, own_ref, other_ref, w_ref, g_ref, wpart_ref, pg_ref, whole):
    core = core_ref[0]
    feats = own_ref.shape[1]
    for i in range(own_ref.shape[0]):
        for ref, c in ((own_ref, core), (other_ref, 1 - core)):
            start = pl.multiple_of((2 * i + c) * feats, feats)
            whole[pl.ds(start, feats), :] = ref[i]
    pre = lax.dot_general(
        whole[...], w_ref[...], (((0,), (0,)), ((), ())), preferred_element_type=F32
    )
    pg = (g_ref[...].astype(F32) * gelu_slope(pre)).astype(BF16)
    pg_ref[...] = pg
    step = 256
    for i in range(whole.shape[0] // step):
        rows = pl.ds(i * step, step)
        wpart_ref[rows, :] = jnp.dot(
            whole[rows, :], pg, preferred_element_type=F32
        ).astype(BF16)


def input_kernel(core_ref, w_ref, pg_ref, keep_ref, send_ref):
    core = core_ref[0]
    pg = pg_ref[...]
    feats = keep_ref.shape[1]
    for i in range(keep_ref.shape[0]):
        for ref, c in ((send_ref, 1 - core), (keep_ref, core)):
            start = pl.multiple_of((2 * i + c) * feats, feats)
            ref[i] = lax.dot_general(
                w_ref[pl.ds(start, feats), :],
                pg,
                (((1,), (1,)), ((), ())),
                preferred_element_type=F32,
            ).astype(ref.dtype)


def local(tokens, w_in, hidden_grad):
    rows, feats = tokens.shape
    d, hidden = w_in.shape
    core = jnp.full((1,), lax.axis_index("c"), jnp.int32)
    swap = [(0, 1), (1, 0)]
    pair = lax.all_gather(tokens.T, "xl", axis=0)
    own = lax.all_gather(pair, "y", axis=0).reshape(16, feats, rows)
    other = lax.ppermute(own, "c", swap)
    wpart, pre_grad = pl.pallas_call(
        hidden_kernel,
        out_shape=(
            jax.ShapeDtypeStruct((d, hidden), BF16),
            jax.ShapeDtypeStruct((rows, hidden), BF16),
        ),
        in_specs=[SMEM, VMEM, VMEM, VMEM, VMEM],
        out_specs=(VMEM, VMEM),
        scratch_shapes=[pltpu.VMEM((d, rows), BF16)],
        compiler_params=pltpu.CompilerParams(vmem_limit_bytes=40 << 20),
        cost_estimate=pl.CostEstimate(
            flops=4 * d * rows * hidden, bytes_accessed=8 << 20, transcendentals=rows * hidden
        ),
    )(core, own, other, w_in, hidden_grad)
    pieces = lax.all_to_all(wpart.reshape(32, feats, hidden), DP, 0, 0, tiled=True)
    keep, send = pl.pallas_call(
        input_kernel,
        out_shape=(
            jax.ShapeDtypeStruct((16, feats, rows), F32),
            jax.ShapeDtypeStruct((16, feats, rows), BF16),
        ),
        in_specs=[SMEM, VMEM, VMEM],
        out_specs=(VMEM, VMEM),
        compiler_params=pltpu.CompilerParams(vmem_limit_bytes=40 << 20),
        cost_estimate=pl.CostEstimate(
            flops=2 * d * rows * hidden, bytes_accessed=5 << 20, transcendentals=0
        ),
    )(core, w_in, pre_grad)
    arrived = lax.ppermute(send, "c", swap)
    both = (keep + arrived.astype(F32)).reshape(16 * feats, rows)
    input_sum = lax.psum_scatter(both, ("y", "xl"), scatter_dimension=0, tiled=True)
    weight_sum = jnp.sum(pieces.astype(F32), axis=0)
    return (input_sum.astype(BF16).T, weight_sum.astype(BF16))


def solution(mesh):
    split = Mesh(mesh.devices.reshape(8, 4, 8, 2, 2), DP + MP)
    return jax.shard_map(
        local,
        mesh=split,
        in_specs=(P(DP, MP), P(None, MP), P(DP, MP)),
        out_specs=(P(DP, MP), P(DP, MP)),
        check_vma=False,
    )
```

```python
import jax
import jax.numpy as jnp
from jax import lax
from jax.experimental import pallas as pl
from jax.experimental.pallas import tpu as pltpu
from jax.sharding import Mesh, PartitionSpec as P

DP = ("z", "xh")
MP = ("y", "xl", "c")
F32 = jnp.float32
BF16 = jnp.bfloat16
VMEM = pl.BlockSpec(memory_space=pltpu.VMEM)
SMEM = pl.BlockSpec(memory_space=pltpu.SMEM)
PAIR = [(0, 1), (1, 0)]


def gelu_slope(pre):
    coef = 0.7978845608028654
    inner = coef * (pre + 0.044715 * pre * pre * pre)
    tval = jnp.tanh(inner)
    return 0.5 * (1.0 + tval) + 0.5 * pre * (1.0 - tval * tval) * coef * (
        1.0 + 3.0 * 0.044715 * pre * pre
    )


def hidden_kernel(at_ref, own_ref, mine_ref, other_ref, w_ref, g_ref, wpart_ref, pg_ref, whole):
    xl, core = at_ref[1], at_ref[2]
    feats = own_ref.shape[2]

    def put(y, x, c, block):
        start = pl.multiple_of((4 * y + 2 * x + c) * feats, feats)
        whole[pl.ds(start, feats), :] = block

    for y in range(own_ref.shape[0]):
        put(y, xl, 0, own_ref[y, 0])
        put(y, xl, 1, own_ref[y, 1])
        put(y, 1 - xl, core, mine_ref[y])
        put(y, 1 - xl, 1 - core, other_ref[y])
    pre = lax.dot_general(
        whole[...], w_ref[...], (((0,), (0,)), ((), ())), preferred_element_type=F32
    )
    pg = (g_ref[...].astype(F32) * gelu_slope(pre)).astype(BF16)
    pg_ref[...] = pg
    step = whole.shape[0] // 12
    for i in range(12):
        rows = pl.ds(i * step, step)
        wpart_ref[rows, :] = jnp.dot(
            whole[rows, :], pg, preferred_element_type=F32
        ).astype(BF16)


def input_kernel(at_ref, w_ref, pg_ref, keep_ref, send_ref):
    y_own, xl, core = at_ref[0], at_ref[1], at_ref[2]
    pg = pg_ref[...]
    feats = keep_ref.shape[1]
    blocks = keep_ref.shape[0]
    ny = blocks // 2
    bits = ny.bit_length() - 1
    for ref, c in ((send_ref, 1 - core), (keep_ref, core)):
        for i in range(blocks):
            x = xl if i < ny else 1 - xl
            r = sum(((i % ny) >> (bits - 1 - k) & 1) << k for k in range(bits))
            start = (4 * lax.bitwise_xor(y_own, jnp.int32(r)) + 2 * x + c) * feats
            ref[i] = lax.dot_general(
                w_ref[pl.ds(pl.multiple_of(start, feats), feats), :],
                pg,
                (((1,), (1,)), ((), ())),
                preferred_element_type=F32,
            ).astype(ref.dtype)


def make_local(nz, nx, ny):
    def local(tokens, w_in, hidden_grad):
        rows, feats = tokens.shape
        d, hidden = w_in.shape
        core = lax.axis_index("c")
        at = jnp.stack([lax.axis_index("y"), lax.axis_index("xl"), core]).astype(jnp.int32)
        own = lax.all_gather(tokens.T, ("y", "c"), axis=0).reshape(ny, 2, feats, rows)
        mine = lax.ppermute(lax.dynamic_index_in_dim(own, core, 1, False), "xl", PAIR)
        other = lax.ppermute(mine, "c", PAIR)
        wpart, pre_grad = pl.pallas_call(
            hidden_kernel,
            out_shape=(
                jax.ShapeDtypeStruct((d, hidden), BF16),
                jax.ShapeDtypeStruct((rows, hidden), BF16),
            ),
            in_specs=[SMEM, VMEM, VMEM, VMEM, VMEM, VMEM],
            out_specs=(VMEM, VMEM),
            scratch_shapes=[pltpu.VMEM((d, rows), BF16)],
            compiler_params=pltpu.CompilerParams(vmem_limit_bytes=16 << 20),
            cost_estimate=pl.CostEstimate(
                flops=4 * d * rows * hidden,
                bytes_accessed=8 << 20,
                transcendentals=rows * hidden,
            ),
        )(at, own, mine, other, w_in, hidden_grad)
        pieces = lax.all_to_all(
            wpart.reshape(nz * nx, d // (nz * nx), hidden), DP, 0, 0, tiled=True
        )
        keep, send = pl.pallas_call(
            input_kernel,
            out_shape=(
                jax.ShapeDtypeStruct((2 * ny, feats, rows), F32),
                jax.ShapeDtypeStruct((2 * ny, feats, rows), BF16),
            ),
            in_specs=[SMEM, VMEM, VMEM],
            out_specs=(VMEM, VMEM),
            compiler_params=pltpu.CompilerParams(vmem_limit_bytes=12 << 20),
            cost_estimate=pl.CostEstimate(
                flops=2 * d * rows * hidden, bytes_accessed=5 << 20, transcendentals=0
            ),
        )(at, w_in, pre_grad)
        total = keep + lax.ppermute(send, "c", PAIR).astype(F32)
        steps = [("xl", PAIR)]
        bit = 1
        while bit < ny:
            steps.append(("y", [(i, i ^ bit) for i in range(ny)]))
            bit *= 2
        for axis, pairs in steps:
            half = total.shape[0] // 2
            arrived = lax.ppermute(total[half:].astype(BF16), axis, pairs)
            total = total[:half] + arrived.astype(F32)
        weight_sum = jnp.sum(pieces.astype(F32), axis=0)
        return (total[0].astype(BF16).T, weight_sum.astype(BF16))

    return local


def solution(mesh, sizes=(8, 4, 8)):
    split = Mesh(mesh.devices.reshape(*sizes, 2, 2), DP + MP)
    return jax.shard_map(
        make_local(*sizes),
        mesh=split,
        in_specs=(P(DP, MP), P(None, MP), P(DP, MP)),
        out_specs=(P(DP, MP), P(DP, MP)),
        check_vma=False,
    )
```

```python
import jax
import jax.numpy as jnp
from jax import lax
from jax.experimental import pallas as pl
from jax.experimental.pallas import tpu as pltpu
from jax.sharding import Mesh, PartitionSpec as P

DP = ("zh", "zl", "xh")
MP = ("y", "xl", "c")
F32 = jnp.float32
BF16 = jnp.bfloat16
VMEM = pl.BlockSpec(memory_space=pltpu.VMEM)
SMEM = pl.BlockSpec(memory_space=pltpu.SMEM)
PAIR = [(0, 1), (1, 0)]


def gelu_slope(pre):
    coef = 0.7978845608028654
    inner = coef * (pre + 0.044715 * pre * pre * pre)
    tval = jnp.tanh(inner)
    return 0.5 * (1.0 + tval) + 0.5 * pre * (1.0 - tval * tval) * coef * (
        1.0 + 3.0 * 0.044715 * pre * pre
    )


def hidden_kernel(
    at_ref, own_ref, mine_ref, other_ref, w_hbm, g_ref, whole, pg_ref, keep_ref, send_ref, w_ref, sem
):
    load = pltpu.make_async_copy(w_hbm, w_ref, sem)
    load.start()
    y_own, xl, core = at_ref[0], at_ref[1], at_ref[2]
    ny, _, feats, _ = own_ref.shape
    bits = ny.bit_length() - 1

    def put(y, x, c, block):
        start = pl.multiple_of((4 * y + 2 * x + c) * feats, feats)
        whole[pl.ds(start, feats), :] = block

    for y in range(ny):
        put(y, xl, 0, own_ref[y, 0])
        put(y, xl, 1, own_ref[y, 1])
        put(y, 1 - xl, core, mine_ref[y])
        put(y, 1 - xl, 1 - core, other_ref[y])
    load.wait()
    pre = lax.dot_general(
        whole[...], w_ref[...], (((0,), (0,)), ((), ())), preferred_element_type=F32
    )
    pg = (g_ref[...].astype(F32) * gelu_slope(pre)).astype(BF16)
    pg_ref[...] = pg
    for r in range(ny):
        at = sum((r >> k & 1) << (bits - 1 - k) for k in range(bits))
        start = lax.bitwise_xor(y_own, jnp.int32(r)) * (4 * feats)
        block = lax.dot_general(
            w_ref[pl.ds(pl.multiple_of(start, 4 * feats), 4 * feats), :],
            pg,
            (((1,), (1,)), ((), ())),
            preferred_element_type=F32,
        )
        for c in range(2):

            @pl.when(core == c)
            def _():
                for x in range(2):
                    to = lax.bitwise_xor(xl, jnp.int32(x)) * ny + at
                    for ref, b in ((keep_ref, 2 * x + c), (send_ref, 2 * x + 1 - c)):
                        rows = block[b * feats : (b + 1) * feats]
                        ref[to] = rows.astype(ref.dtype)


def weight_kernel(at_ref, whole, tmine_ref, tother_ref, pg_ref, pgpair_ref, out_ref):
    xl, core, zl = at_ref[1], at_ref[2], at_ref[3]
    feats = tmine_ref.shape[2]
    for i in range(out_ref.shape[0] // 4):
        for x in range(2):
            for ref, c in ((tmine_ref, core), (tother_ref, 1 - core)):
                b = 2 * lax.bitwise_xor(xl, jnp.int32(x)) + c
                start = pl.multiple_of((4 * (2 * i + zl) + b) * feats, feats)
                total = jnp.dot(
                    whole[pl.ds(start, feats), :], pg_ref[...], preferred_element_type=F32
                ) + jnp.dot(ref[x, i], pgpair_ref[...], preferred_element_type=F32)
                out_ref[4 * i + b] = total.astype(BF16)


def halve(total, axis, pairs):
    half = total.shape[0] // 2
    arrived = lax.ppermute(total[half:].astype(BF16), axis, pairs)
    return total[:half] + arrived.astype(F32)


def make_local(nz, nx, ny):
    nh = nz // 2

    def local(tokens, w_in, hidden_grad):
        rows, feats = tokens.shape
        d, hidden = w_in.shape
        core, zl = lax.axis_index("c"), lax.axis_index("zl")
        at = jnp.stack([lax.axis_index("y"), lax.axis_index("xl"), core, zl]).astype(jnp.int32)

        def pick(array, index, axis):
            return lax.dynamic_index_in_dim(array, index, axis, keepdims=False)

        own = lax.all_gather(tokens.T, ("y", "c"), axis=0).reshape(ny, 2, feats, rows)
        half = pick(own, core, 1)
        mine = lax.ppermute(half, "xl", PAIR)
        other = lax.ppermute(mine, "c", PAIR)
        forth = jnp.stack(
            [pick(a.reshape(nh, 2, feats, rows), 1 - zl, 1) for a in (half, mine)]
        )
        tmine = lax.ppermute(forth, "zl", PAIR)
        tother = lax.ppermute(tmine, "c", PAIR)
        whole, pre_grad, keep, send = pl.pallas_call(
            hidden_kernel,
            out_shape=(
                jax.ShapeDtypeStruct((d, rows), BF16),
                jax.ShapeDtypeStruct((rows, hidden), BF16),
                jax.ShapeDtypeStruct((2 * ny, feats, rows), F32),
                jax.ShapeDtypeStruct((2 * ny, feats, rows), BF16),
            ),
            in_specs=[SMEM, VMEM, VMEM, VMEM, pl.BlockSpec(memory_space=pltpu.HBM), VMEM],
            out_specs=(VMEM, VMEM, VMEM, VMEM),
            scratch_shapes=[pltpu.VMEM((d, hidden), BF16), pltpu.SemaphoreType.DMA],
            compiler_params=pltpu.CompilerParams(vmem_limit_bytes=8 << 20),
            cost_estimate=pl.CostEstimate(
                flops=4 * d * rows * hidden,
                bytes_accessed=8 << 20,
                transcendentals=rows * hidden,
            ),
        )(at, own, mine, other, w_in, hidden_grad)
        pair_grad = lax.ppermute(pre_grad, "zl", PAIR)
        total = keep + lax.ppermute(send, "c", PAIR).astype(F32)
        total = halve(total, "xl", PAIR)
        total, tother = lax.optimization_barrier((total, tother))
        wpart = pl.pallas_call(
            weight_kernel,
            out_shape=jax.ShapeDtypeStruct((4 * nh, feats, hidden), BF16),
            in_specs=[SMEM, VMEM, VMEM, VMEM, VMEM, VMEM],
            out_specs=VMEM,
            compiler_params=pltpu.CompilerParams(vmem_limit_bytes=4 << 20),
            cost_estimate=pl.CostEstimate(
                flops=2 * d * rows * hidden, bytes_accessed=4 << 20, transcendentals=0
            ),
        )(at, whole, tmine, tother, pre_grad, pair_grad)
        wpart = wpart.reshape(nh * nx, -1, hidden)
        pieces = lax.all_to_all(wpart, ("zh", "xh"), 0, 0, tiled=True)
        bit = 1
        while bit < ny:
            total = halve(total, "y", [(i, i ^ bit) for i in range(ny)])
            bit *= 2
        weight_sum = jnp.sum(pieces.astype(F32), axis=0)
        return (total[0].astype(BF16).T, weight_sum.astype(BF16))

    return local


def solution(mesh, sizes=(8, 4, 8)):
    nz, nx, ny = sizes
    split = Mesh(mesh.devices.reshape(nz // 2, 2, nx, ny, 2, 2), DP + MP)
    return jax.shard_map(
        make_local(*sizes),
        mesh=split,
        in_specs=(P(DP, MP), P(None, MP), P(DP, MP)),
        out_specs=(P(DP, MP), P(DP, MP)),
        check_vma=False,
    )
```

```python
import jax
import jax.numpy as jnp
from jax import lax
from jax.experimental import pallas as pl
from jax.experimental.pallas import tpu as pltpu
from jax.sharding import Mesh, PartitionSpec as P

DP = ("zh", "zl", "xh")
MP = ("y", "xl", "c")
F32 = jnp.float32
BF16 = jnp.bfloat16
VMEM = pl.BlockSpec(memory_space=pltpu.VMEM)
SMEM = pl.BlockSpec(memory_space=pltpu.SMEM)
PAIR = [(0, 1), (1, 0)]


def gelu_slope(pre):
    coef = 0.7978845608028654
    inner = coef * (pre + 0.044715 * pre * pre * pre)
    tval = jnp.tanh(inner)
    return 0.5 * (1.0 + tval) + 0.5 * pre * (1.0 - tval * tval) * coef * (
        1.0 + 3.0 * 0.044715 * pre * pre
    )


def hidden_kernel(
    at_ref, own_ref, mine_ref, other_ref, w_ref, g_ref, whole, pg_ref, keep_ref, send_ref
):
    y_own, xl, core = at_ref[0], at_ref[1], at_ref[2]
    ny, _, feats, _ = own_ref.shape
    bits = ny.bit_length() - 1

    def put(y, x, c, block):
        start = pl.multiple_of((4 * y + 2 * x + c) * feats, feats)
        whole[pl.ds(start, feats), :] = block

    for y in range(ny):
        put(y, xl, 0, own_ref[y, 0])
        put(y, xl, 1, own_ref[y, 1])
        put(y, 1 - xl, core, mine_ref[y])
        put(y, 1 - xl, 1 - core, other_ref[y])
    pre = lax.dot_general(
        whole[...], w_ref[...], (((0,), (0,)), ((), ())), preferred_element_type=F32
    )
    pg = (g_ref[...].astype(F32) * gelu_slope(pre)).astype(BF16)
    pg_ref[...] = pg
    for r in range(ny):
        at = sum((r >> k & 1) << (bits - 1 - k) for k in range(bits))
        start = lax.bitwise_xor(y_own, jnp.int32(r)) * (4 * feats)
        block = lax.dot_general(
            w_ref[pl.ds(pl.multiple_of(start, 4 * feats), 4 * feats), :],
            pg,
            (((1,), (1,)), ((), ())),
            preferred_element_type=F32,
        )
        for c in range(2):

            @pl.when(core == c)
            def _():
                for x in range(2):
                    to = 2 * at + lax.bitwise_xor(xl, jnp.int32(x))
                    for ref, b in ((keep_ref, 2 * x + c), (send_ref, 2 * x + 1 - c)):
                        rows = block[b * feats : (b + 1) * feats]
                        ref[to] = rows.astype(ref.dtype)


def weight_kernel(at_ref, whole, tmine_ref, tother_ref, pg_ref, pgpair_ref, out_ref):
    xl, core, zl = at_ref[1], at_ref[2], at_ref[3]
    feats = tmine_ref.shape[2]
    for i in range(out_ref.shape[0] // 4):
        for x in range(2):
            for ref, c in ((tmine_ref, core), (tother_ref, 1 - core)):
                b = 2 * lax.bitwise_xor(xl, jnp.int32(x)) + c
                start = pl.multiple_of((4 * (2 * i + zl) + b) * feats, feats)
                total = jnp.dot(
                    whole[pl.ds(start, feats), :], pg_ref[...], preferred_element_type=F32
                ) + jnp.dot(ref[x, i], pgpair_ref[...], preferred_element_type=F32)
                out_ref[4 * i + b] = total.astype(BF16)


def halve(total, axis, pairs):
    half = total.shape[0] // 2
    arrived = lax.ppermute(total[half:].astype(BF16), axis, pairs)
    return total[:half] + arrived.astype(F32)


def make_local(nz, nx, ny):
    nh = nz // 2

    def local(tokens, w_in, hidden_grad):
        rows, feats = tokens.shape
        d, hidden = w_in.shape
        core, zl = lax.axis_index("c"), lax.axis_index("zl")
        at = jnp.stack([lax.axis_index("y"), lax.axis_index("xl"), core, zl]).astype(jnp.int32)

        def pick(array, index, axis):
            return lax.dynamic_index_in_dim(array, index, axis, keepdims=False)

        own = lax.all_gather(tokens.T, ("y", "c"), axis=0).reshape(ny, 2, feats, rows)
        half = pick(own, core, 1)
        mine = lax.ppermute(half, "xl", PAIR)
        other = lax.ppermute(mine, "c", PAIR)
        forth = jnp.stack(
            [pick(a.reshape(nh, 2, feats, rows), 1 - zl, 1) for a in (half, mine)]
        )
        tmine = lax.ppermute(forth, "zl", PAIR)
        whole, pre_grad, keep, send = pl.pallas_call(
            hidden_kernel,
            out_shape=(
                jax.ShapeDtypeStruct((d, rows), BF16),
                jax.ShapeDtypeStruct((rows, hidden), BF16),
                jax.ShapeDtypeStruct((2 * ny, feats, rows), F32),
                jax.ShapeDtypeStruct((2 * ny, feats, rows), BF16),
            ),
            in_specs=[SMEM, VMEM, VMEM, VMEM, VMEM, VMEM],
            out_specs=(VMEM, VMEM, VMEM, VMEM),
            compiler_params=pltpu.CompilerParams(vmem_limit_bytes=8 << 20),
            cost_estimate=pl.CostEstimate(
                flops=4 * d * rows * hidden,
                bytes_accessed=8 << 20,
                transcendentals=rows * hidden,
            ),
        )(at, own, mine, other, w_in, hidden_grad)
        pre_grad, send, tmine = lax.optimization_barrier((pre_grad, send, tmine))
        pair_grad = lax.ppermute(pre_grad, "zl", PAIR)
        tother = lax.ppermute(tmine, "c", PAIR)
        total = keep + lax.ppermute(send, "c", PAIR).astype(F32)
        total, tother = lax.optimization_barrier((total, tother))
        wpart = pl.pallas_call(
            weight_kernel,
            out_shape=jax.ShapeDtypeStruct((4 * nh, feats, hidden), BF16),
            in_specs=[SMEM, VMEM, VMEM, VMEM, VMEM, VMEM],
            out_specs=VMEM,
            compiler_params=pltpu.CompilerParams(vmem_limit_bytes=4 << 20),
            cost_estimate=pl.CostEstimate(
                flops=2 * d * rows * hidden, bytes_accessed=4 << 20, transcendentals=0
            ),
        )(at, whole, tmine, tother, pre_grad, pair_grad)
        wpart = wpart.reshape(nh * nx, -1, hidden)
        pieces = lax.all_to_all(wpart, ("zh", "xh"), 0, 0, tiled=True)
        bit = 1
        while bit < ny:
            total = halve(total, "y", [(i, i ^ bit) for i in range(ny)])
            bit *= 2
        total = halve(total, "xl", PAIR)
        weight_sum = jnp.sum(pieces.astype(F32), axis=0)
        return (total[0].astype(BF16).T, weight_sum.astype(BF16))

    return local


def solution(mesh, sizes=(8, 4, 8)):
    nz, nx, ny = sizes
    split = Mesh(mesh.devices.reshape(nz // 2, 2, nx, ny, 2, 2), DP + MP)
    return jax.shard_map(
        make_local(*sizes),
        mesh=split,
        in_specs=(P(DP, MP), P(None, MP), P(DP, MP)),
        out_specs=(P(DP, MP), P(DP, MP)),
        check_vma=False,
    )
```

```python
import jax
import jax.numpy as jnp
from jax import lax
from jax.experimental import pallas as pl
from jax.experimental.pallas import tpu as pltpu
from jax.sharding import Mesh, PartitionSpec as P

DP = ("zh", "zl", "xh")
MP = ("y", "xl", "c")
F32 = jnp.float32
BF16 = jnp.bfloat16
VMEM = pl.BlockSpec(memory_space=pltpu.VMEM)
SMEM = pl.BlockSpec(memory_space=pltpu.SMEM)
PAIR = [(0, 1), (1, 0)]


def gelu_slope(pre):
    coef = 0.7978845608028654
    inner = coef * (pre + 0.044715 * pre * pre * pre)
    tval = jnp.tanh(inner)
    return 0.5 * (1.0 + tval) + 0.5 * pre * (1.0 - tval * tval) * coef * (
        1.0 + 3.0 * 0.044715 * pre * pre
    )


def pre_kernel(at_ref, tok_ref, w_ref, pre_ref, w_half):
    pre_ref[...] = half_pre(at_ref[1], tok_ref, w_ref, w_half)


def half_pre(x, tok_ref, w_ref, w_half):
    ny, _, feats, rows = tok_ref.shape
    for y in range(ny):
        start = pl.multiple_of((4 * y + 2 * x) * feats, 2 * feats)
        w_half[pl.ds(2 * y * feats, 2 * feats), :] = w_ref[pl.ds(start, 2 * feats), :]
    return lax.dot_general(
        tok_ref[...].reshape(2 * ny * feats, rows),
        w_half[...],
        (((0,), (0,)), ((), ())),
        preferred_element_type=F32,
    )


def hidden_kernel(
    at_ref, mine_ref, other_ref, w_ref, g_ref, pre_ref, rest, pg_ref, keep_ref, send_ref, w_half
):
    y_own, xl, core = at_ref[0], at_ref[1], at_ref[2]
    ny, feats, _ = mine_ref.shape
    bits = ny.bit_length() - 1
    for y in range(ny):
        rest[y, core] = mine_ref[y]
        rest[y, 1 - core] = other_ref[y]
    pre = pre_ref[...] + half_pre(1 - xl, rest, w_ref, w_half)
    pg = (g_ref[...].astype(F32) * gelu_slope(pre)).astype(BF16)
    pg_ref[...] = pg
    for r in range(ny):
        at = sum((r >> k & 1) << (bits - 1 - k) for k in range(bits))
        start = lax.bitwise_xor(y_own, jnp.int32(r)) * (4 * feats)
        block = lax.dot_general(
            w_ref[pl.ds(pl.multiple_of(start, 4 * feats), 4 * feats), :],
            pg,
            (((1,), (1,)), ((), ())),
            preferred_element_type=F32,
        )
        for c in range(2):

            @pl.when(core == c)
            def _():
                for x in range(2):
                    to = lax.bitwise_xor(xl, jnp.int32(x)) * ny + at
                    for ref, b in ((keep_ref, 2 * x + c), (send_ref, 2 * x + 1 - c)):
                        part = block[b * feats : (b + 1) * feats]
                        ref[to] = part.astype(ref.dtype)


def weight_kernel(at_ref, own, rest, t1_ref, t2_ref, tother_ref, pg_ref, pgpair_ref, out_ref):
    xl, core, zl = at_ref[1], at_ref[2], at_ref[3]
    nh = t1_ref.shape[0]
    for i in range(nh):
        for x, (tok, mine) in enumerate(((own, t1_ref), (rest, t2_ref))):
            for c, pair in ((core, mine[i]), (1 - core, tother_ref[x * nh + i])):
                total = jnp.dot(
                    tok[2 * i + zl, c], pg_ref[...], preferred_element_type=F32
                ) + jnp.dot(pair, pgpair_ref[...], preferred_element_type=F32)
                out_ref[4 * i + 2 * lax.bitwise_xor(xl, jnp.int32(x)) + c] = total.astype(BF16)


def halve(total, axis, pairs):
    half = total.shape[0] // 2
    arrived = lax.ppermute(total[half:].astype(BF16), axis, pairs)
    return total[:half] + arrived.astype(F32)


def make_local(nz, nx, ny):
    nh = nz // 2

    def local(tokens, w_in, hidden_grad):
        rows, feats = tokens.shape
        d, hidden = w_in.shape
        core, zl = lax.axis_index("c"), lax.axis_index("zl")
        at = jnp.stack([lax.axis_index("y"), lax.axis_index("xl"), core, zl]).astype(jnp.int32)

        def pick(array, index, axis):
            return lax.dynamic_index_in_dim(array, index, axis, keepdims=False)

        own = lax.all_gather(tokens.T, ("y", "c"), axis=0).reshape(ny, 2, feats, rows)
        half = pick(own, core, 1)
        mine = lax.ppermute(half, "xl", PAIR)
        t1 = lax.ppermute(pick(half.reshape(nh, 2, feats, rows), 1 - zl, 1), "zl", PAIR)
        pre = pl.pallas_call(
            pre_kernel,
            out_shape=jax.ShapeDtypeStruct((rows, hidden), F32),
            in_specs=[SMEM, VMEM, VMEM],
            out_specs=VMEM,
            scratch_shapes=[pltpu.VMEM((d // 2, hidden), BF16)],
            compiler_params=pltpu.CompilerParams(vmem_limit_bytes=8 << 20),
            cost_estimate=pl.CostEstimate(
                flops=d * rows * hidden, bytes_accessed=4 << 20, transcendentals=0
            ),
        )(at, own, w_in)
        mine, t1, pre = lax.optimization_barrier((mine, t1, pre))
        other = lax.ppermute(mine, "c", PAIR)
        t2 = lax.ppermute(pick(mine.reshape(nh, 2, feats, rows), 1 - zl, 1), "zl", PAIR)
        rest, pre_grad, keep, send = pl.pallas_call(
            hidden_kernel,
            out_shape=(
                jax.ShapeDtypeStruct((ny, 2, feats, rows), BF16),
                jax.ShapeDtypeStruct((rows, hidden), BF16),
                jax.ShapeDtypeStruct((2 * ny, feats, rows), F32),
                jax.ShapeDtypeStruct((2 * ny, feats, rows), BF16),
            ),
            in_specs=[SMEM, VMEM, VMEM, VMEM, VMEM, VMEM],
            out_specs=(VMEM, VMEM, VMEM, VMEM),
            scratch_shapes=[pltpu.VMEM((d // 2, hidden), BF16)],
            compiler_params=pltpu.CompilerParams(vmem_limit_bytes=8 << 20),
            cost_estimate=pl.CostEstimate(
                flops=3 * d * rows * hidden,
                bytes_accessed=8 << 20,
                transcendentals=rows * hidden,
            ),
        )(at, mine, other, w_in, hidden_grad, pre)
        pre_grad, send, t1, t2 = lax.optimization_barrier((pre_grad, send, t1, t2))
        pair_grad = lax.ppermute(pre_grad, "zl", PAIR)
        swapped = lax.ppermute(jnp.concatenate([send, t1, t2]), "c", PAIR)
        total = keep + swapped[: 2 * ny].astype(F32)
        total, tother = lax.optimization_barrier((total, swapped[2 * ny :]))
        wpart = pl.pallas_call(
            weight_kernel,
            out_shape=jax.ShapeDtypeStruct((4 * nh, feats, hidden), BF16),
            in_specs=[SMEM] + [VMEM] * 7,
            out_specs=VMEM,
            compiler_params=pltpu.CompilerParams(vmem_limit_bytes=4 << 20),
            cost_estimate=pl.CostEstimate(
                flops=2 * d * rows * hidden, bytes_accessed=4 << 20, transcendentals=0
            ),
        )(at, own, rest, t1, t2, tother, pre_grad, pair_grad)
        pieces = lax.all_to_all(wpart.reshape(nh, -1, hidden), "zh", 0, 0, tiled=True)
        steps = [("xl", PAIR)]
        bit = 1
        while bit < ny:
            steps.append(("y", [(i, i ^ bit) for i in range(ny)]))
            bit *= 2
        for n, (axis, pairs) in enumerate(steps):
            if n == len(steps) - 1:
                total, pieces = lax.optimization_barrier((total, pieces))
            total = halve(total, axis, pairs)
        sums = jnp.sum(pieces.astype(F32), axis=0).astype(BF16)
        pieces = lax.all_to_all(sums.reshape(nx, -1, hidden), "xh", 0, 0, tiled=True)
        weight_sum = jnp.sum(pieces.astype(F32), axis=0)
        return (total[0].astype(BF16).T, weight_sum.astype(BF16))

    return local


def solution(mesh, sizes=(8, 4, 8)):
    nz, nx, ny = sizes
    split = Mesh(mesh.devices.reshape(nz // 2, 2, nx, ny, 2, 2), DP + MP)
    return jax.shard_map(
        make_local(*sizes),
        mesh=split,
        in_specs=(P(DP, MP), P(None, MP), P(DP, MP)),
        out_specs=(P(DP, MP), P(DP, MP)),
        check_vma=False,
    )
```

```python
import jax
import jax.numpy as jnp
from jax import lax
from jax.experimental import pallas as pl
from jax.experimental.pallas import tpu as pltpu
from jax.sharding import Mesh, PartitionSpec as P

DP = ("zh", "zl", "xh")
MP = ("y", "xl", "c")
F32 = jnp.float32
BF16 = jnp.bfloat16
VMEM = pl.BlockSpec(memory_space=pltpu.VMEM)
SMEM = pl.BlockSpec(memory_space=pltpu.SMEM)
PAIR = [(0, 1), (1, 0)]
EARLY_FLOPS = 60_000_000_000


def gelu_slope(pre):
    coef = 0.7978845608028654
    inner = coef * (pre + 0.044715 * pre * pre * pre)
    tval = jnp.tanh(inner)
    return 0.5 * (1.0 + tval) + 0.5 * pre * (1.0 - tval * tval) * coef * (
        1.0 + 3.0 * 0.044715 * pre * pre
    )


def pre_kernel(at_ref, tok_ref, w_ref, pre_ref, w_half):
    pre_ref[...] = half_pre(at_ref[1], tok_ref, w_ref, w_half)


def half_pre(x, tok_ref, w_ref, w_half):
    ny, _, feats, rows = tok_ref.shape
    for y in range(ny):
        start = pl.multiple_of((4 * y + 2 * x) * feats, 2 * feats)
        w_half[pl.ds(2 * y * feats, 2 * feats), :] = w_ref[pl.ds(start, 2 * feats), :]
    return lax.dot_general(
        tok_ref[...].reshape(2 * ny * feats, rows),
        w_half[...],
        (((0,), (0,)), ((), ())),
        preferred_element_type=F32,
    )


def hidden_kernel(
    at_ref, mine_ref, other_ref, w_ref, g_ref, pre_ref, rest, pg_ref, w_half
):
    xl, core = at_ref[1], at_ref[2]
    for y in range(mine_ref.shape[0]):
        rest[y, core] = mine_ref[y]
        rest[y, 1 - core] = other_ref[y]
    pre = pre_ref[...] + half_pre(1 - xl, rest, w_ref, w_half)
    pg_ref[...] = (g_ref[...].astype(F32) * gelu_slope(pre)).astype(BF16)


def input_kernel(at_ref, w_ref, pg_ref, keep_ref, send_ref):
    y_own, xl, core = at_ref[0], at_ref[1], at_ref[2]
    ny, feats = keep_ref.shape[0] // 2, keep_ref.shape[1]
    bits = ny.bit_length() - 1
    pg = pg_ref[...]
    for r in range(ny):
        at = sum((r >> k & 1) << (bits - 1 - k) for k in range(bits))
        start = lax.bitwise_xor(y_own, jnp.int32(r)) * (4 * feats)
        block = lax.dot_general(
            w_ref[pl.ds(pl.multiple_of(start, 4 * feats), 4 * feats), :],
            pg,
            (((1,), (1,)), ((), ())),
            preferred_element_type=F32,
        )
        for c in range(2):

            @pl.when(core == c)
            def _():
                for x in range(2):
                    to = lax.bitwise_xor(xl, jnp.int32(x)) * ny + at
                    for ref, b in ((keep_ref, 2 * x + c), (send_ref, 2 * x + 1 - c)):
                        part = block[b * feats : (b + 1) * feats]
                        ref[to] = part.astype(ref.dtype)


def own_kernel(at_ref, own, rest, pg_ref, acc_ref):
    xl, core, zl = at_ref[1], at_ref[2], at_ref[3]
    for i in range(acc_ref.shape[0] // 4):
        for x, tok in ((xl, own), (1 - xl, rest)):
            for c in (core, 1 - core):
                acc_ref[4 * i + 2 * x + c] = jnp.dot(
                    tok[2 * i + zl, c], pg_ref[...], preferred_element_type=F32
                )


def weight_kernel(at_ref, acc_ref, t1_ref, t2_ref, tother_ref, pgpair_ref, out_ref):
    xl, core = at_ref[1], at_ref[2]
    nh = t1_ref.shape[0]
    for i in range(nh):
        for x, mine in ((0, t1_ref), (1, t2_ref)):
            for c, tok in ((core, mine[i]), (1 - core, tother_ref[x * nh + i])):
                at = 4 * i + 2 * lax.bitwise_xor(xl, jnp.int32(x)) + c
                total = acc_ref[at] + jnp.dot(
                    tok, pgpair_ref[...], preferred_element_type=F32
                )
                out_ref[at] = total.astype(BF16)


def add_kernel(keep_ref, arrived_ref, out_ref):
    out_ref[...] = keep_ref[...] + arrived_ref[...].astype(F32)


def halve_early(total, axis, pairs):
    half = total.shape[0] // 2
    arrived = lax.ppermute(total[half:].astype(BF16), axis, pairs)
    return pl.pallas_call(
        add_kernel,
        out_shape=jax.ShapeDtypeStruct(arrived.shape, F32),
        in_specs=[VMEM, VMEM],
        out_specs=VMEM,
        compiler_params=pltpu.CompilerParams(vmem_limit_bytes=4 << 20),
        cost_estimate=pl.CostEstimate(
            flops=EARLY_FLOPS, bytes_accessed=2 << 20, transcendentals=0
        ),
    )(total[:half], arrived)


def halve(total, axis, pairs):
    half = total.shape[0] // 2
    arrived = lax.ppermute(total[half:].astype(BF16), axis, pairs)
    return total[:half] + arrived.astype(F32)


def make_local(nz, nx, ny):
    nh = nz // 2

    def local(tokens, w_in, hidden_grad):
        rows, feats = tokens.shape
        d, hidden = w_in.shape
        core, zl = lax.axis_index("c"), lax.axis_index("zl")
        at = jnp.stack([lax.axis_index("y"), lax.axis_index("xl"), core, zl]).astype(jnp.int32)

        def pick(array, index, axis):
            return lax.dynamic_index_in_dim(array, index, axis, keepdims=False)

        own = lax.all_gather(tokens.T, ("y", "c"), axis=0).reshape(ny, 2, feats, rows)
        half = pick(own, core, 1)
        mine = lax.ppermute(half, "xl", PAIR)
        t1 = lax.ppermute(pick(half.reshape(nh, 2, feats, rows), 1 - zl, 1), "zl", PAIR)
        pre = pl.pallas_call(
            pre_kernel,
            out_shape=jax.ShapeDtypeStruct((rows, hidden), F32),
            in_specs=[SMEM, VMEM, VMEM],
            out_specs=VMEM,
            scratch_shapes=[pltpu.VMEM((d // 2, hidden), BF16)],
            compiler_params=pltpu.CompilerParams(vmem_limit_bytes=8 << 20),
            cost_estimate=pl.CostEstimate(
                flops=d * rows * hidden, bytes_accessed=4 << 20, transcendentals=0
            ),
        )(at, own, w_in)
        mine, t1, pre = lax.optimization_barrier((mine, t1, pre))
        other = lax.ppermute(mine, "c", PAIR)
        t2 = lax.ppermute(pick(mine.reshape(nh, 2, feats, rows), 1 - zl, 1), "zl", PAIR)
        rest, pre_grad = pl.pallas_call(
            hidden_kernel,
            out_shape=(
                jax.ShapeDtypeStruct((ny, 2, feats, rows), BF16),
                jax.ShapeDtypeStruct((rows, hidden), BF16),
            ),
            in_specs=[SMEM] + [VMEM] * 5,
            out_specs=(VMEM, VMEM),
            scratch_shapes=[pltpu.VMEM((d // 2, hidden), BF16)],
            compiler_params=pltpu.CompilerParams(vmem_limit_bytes=8 << 20),
            cost_estimate=pl.CostEstimate(
                flops=d * rows * hidden,
                bytes_accessed=5 << 20,
                transcendentals=rows * hidden,
            ),
        )(at, mine, other, w_in, hidden_grad, pre)
        pair_grad = lax.ppermute(pre_grad, "zl", PAIR)
        keep, send = pl.pallas_call(
            input_kernel,
            out_shape=(
                jax.ShapeDtypeStruct((2 * ny, feats, rows), F32),
                jax.ShapeDtypeStruct((2 * ny, feats, rows), BF16),
            ),
            in_specs=[SMEM, VMEM, VMEM],
            out_specs=(VMEM, VMEM),
            compiler_params=pltpu.CompilerParams(vmem_limit_bytes=8 << 20),
            cost_estimate=pl.CostEstimate(
                flops=2 * d * rows * hidden, bytes_accessed=5 << 20, transcendentals=0
            ),
        )(at, w_in, pre_grad)
        acc = pl.pallas_call(
            own_kernel,
            out_shape=jax.ShapeDtypeStruct((4 * nh, feats, hidden), F32),
            in_specs=[SMEM] + [VMEM] * 3,
            out_specs=VMEM,
            compiler_params=pltpu.CompilerParams(vmem_limit_bytes=4 << 20),
            cost_estimate=pl.CostEstimate(
                flops=d * rows * hidden, bytes_accessed=4 << 20, transcendentals=0
            ),
        )(at, own, rest, pre_grad)
        send, t1, t2, pair_grad, acc = lax.optimization_barrier((send, t1, t2, pair_grad, acc))
        swapped = lax.ppermute(jnp.concatenate([send, t1, t2]), "c", PAIR)
        total = keep + swapped[: 2 * ny].astype(F32)
        total, tother = lax.optimization_barrier((total, swapped[2 * ny :]))
        wpart = pl.pallas_call(
            weight_kernel,
            out_shape=jax.ShapeDtypeStruct((4 * nh, feats, hidden), BF16),
            in_specs=[SMEM] + [VMEM] * 5,
            out_specs=VMEM,
            compiler_params=pltpu.CompilerParams(vmem_limit_bytes=4 << 20),
            cost_estimate=pl.CostEstimate(
                flops=d * rows * hidden, bytes_accessed=4 << 20, transcendentals=0
            ),
        )(at, acc, t1, t2, tother, pair_grad)
        wpart = wpart.reshape(nh * nx, -1, hidden)
        pieces = lax.all_to_all(wpart, ("zh", "xh"), 0, 0, tiled=True)
        total = halve_early(total, "xl", PAIR)
        bit = 1
        while bit < ny:
            total = halve(total, "y", [(i, i ^ bit) for i in range(ny)])
            bit *= 2
        weight_sum = jnp.sum(pieces.astype(F32), axis=0)
        return (total[0].astype(BF16).T, weight_sum.astype(BF16))

    return local


def solution(mesh, sizes=(8, 4, 8)):
    nz, nx, ny = sizes
    split = Mesh(mesh.devices.reshape(nz // 2, 2, nx, ny, 2, 2), DP + MP)
    return jax.shard_map(
        make_local(*sizes),
        mesh=split,
        in_specs=(P(DP, MP), P(None, MP), P(DP, MP)),
        out_specs=(P(DP, MP), P(DP, MP)),
        check_vma=False,
    )
```

```python
import jax
import jax.numpy as jnp
from jax import lax
from jax.experimental import pallas as pl
from jax.experimental.pallas import tpu as pltpu
from jax.sharding import Mesh, PartitionSpec as P

DP = ("zh", "zl", "xh")
MP = ("y", "xl", "c")
F32 = jnp.float32
BF16 = jnp.bfloat16
VMEM = pl.BlockSpec(memory_space=pltpu.VMEM)
SMEM = pl.BlockSpec(memory_space=pltpu.SMEM)
PAIR = [(0, 1), (1, 0)]
EARLY_FLOPS = 60_000_000_000


def gelu_slope(pre):
    coef = 0.7978845608028654
    inner = coef * (pre + 0.044715 * pre * pre * pre)
    tval = jnp.tanh(inner)
    return 0.5 * (1.0 + tval) + 0.5 * pre * (1.0 - tval * tval) * coef * (
        1.0 + 3.0 * 0.044715 * pre * pre
    )


def pre_kernel(at_ref, tok_ref, w_ref, pre_ref, w_half):
    pre_ref[...] = half_pre(at_ref[1], tok_ref, w_ref, w_half)


def half_pre(x, tok_ref, w_ref, w_half):
    ny, _, feats, rows = tok_ref.shape
    for y in range(ny):
        start = pl.multiple_of((4 * y + 2 * x) * feats, 2 * feats)
        w_half[pl.ds(2 * y * feats, 2 * feats), :] = w_ref[pl.ds(start, 2 * feats), :]
    return lax.dot_general(
        tok_ref[...].reshape(2 * ny * feats, rows),
        w_half[...],
        (((0,), (0,)), ((), ())),
        preferred_element_type=F32,
    )


def hidden_kernel(
    at_ref, mine_ref, other_ref, w_ref, g_ref, pre_ref, rest, pg_ref, w_half
):
    xl, core = at_ref[1], at_ref[2]
    for y in range(mine_ref.shape[0]):
        rest[y, core] = mine_ref[y]
        rest[y, 1 - core] = other_ref[y]
    pre = pre_ref[...] + half_pre(1 - xl, rest, w_ref, w_half)
    pg_ref[...] = (g_ref[...].astype(F32) * gelu_slope(pre)).astype(BF16)


def input_kernel(at_ref, w_ref, pg_ref, t1_ref, t2_ref, keep_ref, send_ref):
    y_own, xl, core = at_ref[0], at_ref[1], at_ref[2]
    ny, feats = keep_ref.shape[0] // 2, keep_ref.shape[1]
    nh = t1_ref.shape[0]
    bits = ny.bit_length() - 1
    send_ref[2 * ny : 2 * ny + nh] = t1_ref[...]
    send_ref[2 * ny + nh :] = t2_ref[...]
    pg = pg_ref[...]
    for r in range(ny):
        at = sum((r >> k & 1) << (bits - 1 - k) for k in range(bits))
        start = lax.bitwise_xor(y_own, jnp.int32(r)) * (4 * feats)
        block = lax.dot_general(
            w_ref[pl.ds(pl.multiple_of(start, 4 * feats), 4 * feats), :],
            pg,
            (((1,), (1,)), ((), ())),
            preferred_element_type=F32,
        )
        for c in range(2):

            @pl.when(core == c)
            def _():
                for x in range(2):
                    to = lax.bitwise_xor(xl, jnp.int32(x)) * ny + at
                    for ref, b in ((keep_ref, 2 * x + c), (send_ref, 2 * x + 1 - c)):
                        part = block[b * feats : (b + 1) * feats]
                        ref[to] = part.astype(ref.dtype)


def own_kernel(at_ref, own, rest, pg_ref, acc_ref):
    xl, core, zl = at_ref[1], at_ref[2], at_ref[3]
    for i in range(acc_ref.shape[0] // 4):
        for x, tok in ((xl, own), (1 - xl, rest)):
            for c in (core, 1 - core):
                acc_ref[4 * i + 2 * x + c] = jnp.dot(
                    tok[2 * i + zl, c], pg_ref[...], preferred_element_type=F32
                )


def weight_kernel(at_ref, acc_ref, t1_ref, t2_ref, tother_ref, pgpair_ref, out_ref):
    xl, core = at_ref[1], at_ref[2]
    nh = t1_ref.shape[0]
    for i in range(nh):
        for x, mine in ((0, t1_ref), (1, t2_ref)):
            for c, tok in ((core, mine[i]), (1 - core, tother_ref[x * nh + i])):
                at = 4 * i + 2 * lax.bitwise_xor(xl, jnp.int32(x)) + c
                total = acc_ref[at] + jnp.dot(
                    tok, pgpair_ref[...], preferred_element_type=F32
                )
                out_ref[at] = total.astype(BF16)


def add_kernel(keep_ref, arrived_ref, out_ref):
    out_ref[...] = keep_ref[...] + arrived_ref[...].astype(F32)


def halve_early(total, axis, pairs):
    half = total.shape[0] // 2
    arrived = lax.ppermute(total[half:].astype(BF16), axis, pairs)
    return pl.pallas_call(
        add_kernel,
        out_shape=jax.ShapeDtypeStruct(arrived.shape, F32),
        in_specs=[VMEM, VMEM],
        out_specs=VMEM,
        compiler_params=pltpu.CompilerParams(vmem_limit_bytes=4 << 20),
        cost_estimate=pl.CostEstimate(
            flops=EARLY_FLOPS, bytes_accessed=2 << 20, transcendentals=0
        ),
    )(total[:half], arrived)


def halve(total, axis, pairs):
    half = total.shape[0] // 2
    arrived = lax.ppermute(total[half:].astype(BF16), axis, pairs)
    return total[:half] + arrived.astype(F32)


def make_local(nz, nx, ny):
    nh = nz // 2

    def local(tokens, w_in, hidden_grad):
        rows, feats = tokens.shape
        d, hidden = w_in.shape
        core, zl = lax.axis_index("c"), lax.axis_index("zl")
        at = jnp.stack([lax.axis_index("y"), lax.axis_index("xl"), core, zl]).astype(jnp.int32)

        def pick(array, index, axis):
            return lax.dynamic_index_in_dim(array, index, axis, keepdims=False)

        own = lax.all_gather(tokens.T, ("y", "c"), axis=0).reshape(ny, 2, feats, rows)
        half = pick(own, core, 1)
        mine = lax.ppermute(half, "xl", PAIR)
        t1 = pick(pick(own.reshape(nh, 2, 2, feats, rows), 1 - zl, 1), core, 1)
        t1 = lax.ppermute(t1, "zl", PAIR)
        pre = pl.pallas_call(
            pre_kernel,
            out_shape=jax.ShapeDtypeStruct((rows, hidden), F32),
            in_specs=[SMEM, VMEM, VMEM],
            out_specs=VMEM,
            scratch_shapes=[pltpu.VMEM((d // 2, hidden), BF16)],
            compiler_params=pltpu.CompilerParams(vmem_limit_bytes=8 << 20),
            cost_estimate=pl.CostEstimate(
                flops=d * rows * hidden, bytes_accessed=4 << 20, transcendentals=0
            ),
        )(at, own, w_in)
        mine, t1, pre = lax.optimization_barrier((mine, t1, pre))
        other = lax.ppermute(mine, "c", PAIR)
        t2 = lax.ppermute(pick(mine.reshape(nh, 2, feats, rows), 1 - zl, 1), "zl", PAIR)
        rest, pre_grad = pl.pallas_call(
            hidden_kernel,
            out_shape=(
                jax.ShapeDtypeStruct((ny, 2, feats, rows), BF16),
                jax.ShapeDtypeStruct((rows, hidden), BF16),
            ),
            in_specs=[SMEM] + [VMEM] * 5,
            out_specs=(VMEM, VMEM),
            scratch_shapes=[pltpu.VMEM((d // 2, hidden), BF16)],
            compiler_params=pltpu.CompilerParams(vmem_limit_bytes=8 << 20),
            cost_estimate=pl.CostEstimate(
                flops=d * rows * hidden,
                bytes_accessed=5 << 20,
                transcendentals=rows * hidden,
            ),
        )(at, mine, other, w_in, hidden_grad, pre)
        pair_grad = lax.ppermute(pre_grad, "zl", PAIR)
        keep, send = pl.pallas_call(
            input_kernel,
            out_shape=(
                jax.ShapeDtypeStruct((2 * ny, feats, rows), F32),
                jax.ShapeDtypeStruct((2 * ny + 2 * nh, feats, rows), BF16),
            ),
            in_specs=[SMEM] + [VMEM] * 4,
            out_specs=(VMEM, VMEM),
            compiler_params=pltpu.CompilerParams(vmem_limit_bytes=8 << 20),
            cost_estimate=pl.CostEstimate(
                flops=2 * d * rows * hidden, bytes_accessed=5 << 20, transcendentals=0
            ),
        )(at, w_in, pre_grad, t1, t2)
        acc = pl.pallas_call(
            own_kernel,
            out_shape=jax.ShapeDtypeStruct((4 * nh, feats, hidden), F32),
            in_specs=[SMEM] + [VMEM] * 3,
            out_specs=VMEM,
            compiler_params=pltpu.CompilerParams(vmem_limit_bytes=4 << 20),
            cost_estimate=pl.CostEstimate(
                flops=d * rows * hidden, bytes_accessed=4 << 20, transcendentals=0
            ),
        )(at, own, rest, pre_grad)
        send, pair_grad, acc = lax.optimization_barrier((send, pair_grad, acc))
        swapped = lax.ppermute(send, "c", PAIR)
        total = keep + swapped[: 2 * ny].astype(F32)
        total, tother = lax.optimization_barrier((total, swapped[2 * ny :]))
        wpart = pl.pallas_call(
            weight_kernel,
            out_shape=jax.ShapeDtypeStruct((4 * nh, feats, hidden), BF16),
            in_specs=[SMEM] + [VMEM] * 5,
            out_specs=VMEM,
            compiler_params=pltpu.CompilerParams(vmem_limit_bytes=4 << 20),
            cost_estimate=pl.CostEstimate(
                flops=d * rows * hidden, bytes_accessed=4 << 20, transcendentals=0
            ),
        )(at, acc, t1, t2, tother, pair_grad)
        wpart = wpart.reshape(nh * nx, -1, hidden)
        pieces = lax.all_to_all(wpart, ("zh", "xh"), 0, 0, tiled=True)
        total = halve_early(total, "xl", PAIR)
        bit = 1
        while bit < ny:
            total = halve(total, "y", [(i, i ^ bit) for i in range(ny)])
            bit *= 2
        weight_sum = jnp.sum(pieces.astype(F32), axis=0)
        return (total[0].astype(BF16).T, weight_sum.astype(BF16))

    return local


def solution(mesh, sizes=(8, 4, 8)):
    nz, nx, ny = sizes
    split = Mesh(mesh.devices.reshape(nz // 2, 2, nx, ny, 2, 2), DP + MP)
    return jax.shard_map(
        make_local(*sizes),
        mesh=split,
        in_specs=(P(DP, MP), P(None, MP), P(DP, MP)),
        out_specs=(P(DP, MP), P(DP, MP)),
        check_vma=False,
    )
```

```python
import jax
import jax.numpy as jnp
from jax import lax
from jax.experimental import pallas as pl
from jax.experimental.pallas import tpu as pltpu
from jax.sharding import Mesh, PartitionSpec as P

DP = ("zh", "zl", "xh")
MP = ("y", "xl", "c")
F32 = jnp.float32
BF16 = jnp.bfloat16
VMEM = pl.BlockSpec(memory_space=pltpu.VMEM)
SMEM = pl.BlockSpec(memory_space=pltpu.SMEM)
PAIR = [(0, 1), (1, 0)]
EARLY_FLOPS = 60_000_000_000


def gelu_slope(pre):
    coef = 0.7978845608028654
    inner = coef * (pre + 0.044715 * pre * pre * pre)
    tval = jnp.tanh(inner)
    return 0.5 * (1.0 + tval) + 0.5 * pre * (1.0 - tval * tval) * coef * (
        1.0 + 3.0 * 0.044715 * pre * pre
    )


def pre_kernel(at_ref, tok_ref, w_ref, pre_ref, w_half):
    pre_ref[...] = half_pre(at_ref[1], tok_ref, w_ref, w_half)


def half_pre(x, tok_ref, w_ref, w_half):
    ny, _, feats, rows = tok_ref.shape
    for y in range(ny):
        start = pl.multiple_of((4 * y + 2 * x) * feats, 2 * feats)
        w_half[pl.ds(2 * y * feats, 2 * feats), :] = w_ref[pl.ds(start, 2 * feats), :]
    return lax.dot_general(
        tok_ref[...].reshape(2 * ny * feats, rows),
        w_half[...],
        (((0,), (0,)), ((), ())),
        preferred_element_type=F32,
    )


def hidden_kernel(
    at_ref, mine_ref, other_ref, w_ref, g_ref, pre_ref, rest, pg_ref, w_half
):
    xl, core = at_ref[1], at_ref[2]
    for y in range(mine_ref.shape[0]):
        rest[y, core] = mine_ref[y]
        rest[y, 1 - core] = other_ref[y]
    pre = pre_ref[...] + half_pre(1 - xl, rest, w_ref, w_half)
    pg_ref[...] = (g_ref[...].astype(F32) * gelu_slope(pre)).astype(BF16)


def input_kernel(at_ref, w_ref, pg_ref, t1_ref, t2_ref, keep_ref, send_ref):
    y_own, xl, core = at_ref[0], at_ref[1], at_ref[2]
    ny, feats = keep_ref.shape[0] // 2, keep_ref.shape[1]
    nh = t1_ref.shape[0]
    bits = ny.bit_length() - 1
    send_ref[2 * ny : 2 * ny + nh] = t1_ref[...]
    send_ref[2 * ny + nh :] = t2_ref[...]
    pg = pg_ref[...]
    for r in range(ny):
        at = sum((r >> k & 1) << (bits - 1 - k) for k in range(bits))
        start = lax.bitwise_xor(y_own, jnp.int32(r)) * (4 * feats)
        block = lax.dot_general(
            w_ref[pl.ds(pl.multiple_of(start, 4 * feats), 4 * feats), :],
            pg,
            (((1,), (1,)), ((), ())),
            preferred_element_type=F32,
        )
        for c in range(2):

            @pl.when(core == c)
            def _():
                for x in range(2):
                    to = 2 * at + lax.bitwise_xor(xl, jnp.int32(x))
                    for ref, b in ((keep_ref, 2 * x + c), (send_ref, 2 * x + 1 - c)):
                        part = block[b * feats : (b + 1) * feats]
                        ref[to] = part.astype(ref.dtype)


def own_kernel(at_ref, own, rest, pg_ref, acc_ref):
    xl, core, zl = at_ref[1], at_ref[2], at_ref[3]
    for i in range(acc_ref.shape[0] // 4):
        for x, tok in ((xl, own), (1 - xl, rest)):
            for c in (core, 1 - core):
                acc_ref[4 * i + 2 * x + c] = jnp.dot(
                    tok[2 * i + zl, c], pg_ref[...], preferred_element_type=F32
                )


def weight_kernel(at_ref, acc_ref, t1_ref, t2_ref, tother_ref, pgpair_ref, out_ref):
    xl, core = at_ref[1], at_ref[2]
    nh = t1_ref.shape[0]
    for i in range(nh):
        for x, mine in ((0, t1_ref), (1, t2_ref)):
            for c, tok in ((core, mine[i]), (1 - core, tother_ref[x * nh + i])):
                at = 4 * i + 2 * lax.bitwise_xor(xl, jnp.int32(x)) + c
                total = acc_ref[at] + jnp.dot(
                    tok, pgpair_ref[...], preferred_element_type=F32
                )
                out_ref[at] = total.astype(BF16)


def add_kernel(keep_ref, arrived_ref, out_ref):
    out_ref[...] = keep_ref[...] + arrived_ref[...].astype(F32)


def halve_early(total, axis, pairs):
    half = total.shape[0] // 2
    arrived = lax.ppermute(total[half:].astype(BF16), axis, pairs)
    return pl.pallas_call(
        add_kernel,
        out_shape=jax.ShapeDtypeStruct(arrived.shape, F32),
        in_specs=[VMEM, VMEM],
        out_specs=VMEM,
        compiler_params=pltpu.CompilerParams(vmem_limit_bytes=4 << 20),
        cost_estimate=pl.CostEstimate(
            flops=EARLY_FLOPS, bytes_accessed=2 << 20, transcendentals=0
        ),
    )(total[:half], arrived)


def halve(total, axis, pairs):
    half = total.shape[0] // 2
    arrived = lax.ppermute(total[half:].astype(BF16), axis, pairs)
    return total[:half] + arrived.astype(F32)


def make_local(nz, nx, ny):
    nh = nz // 2

    def local(tokens, w_in, hidden_grad):
        rows, feats = tokens.shape
        d, hidden = w_in.shape
        core, zl = lax.axis_index("c"), lax.axis_index("zl")
        at = jnp.stack([lax.axis_index("y"), lax.axis_index("xl"), core, zl]).astype(jnp.int32)

        def pick(array, index, axis):
            return lax.dynamic_index_in_dim(array, index, axis, keepdims=False)

        own = lax.all_gather(tokens.T, ("y", "c"), axis=0).reshape(ny, 2, feats, rows)
        half = pick(own, core, 1)
        mine = lax.ppermute(half, "xl", PAIR)
        t1 = pick(pick(own.reshape(nh, 2, 2, feats, rows), 1 - zl, 1), core, 1)
        t1 = lax.ppermute(t1, "zl", PAIR)
        pre = pl.pallas_call(
            pre_kernel,
            out_shape=jax.ShapeDtypeStruct((rows, hidden), F32),
            in_specs=[SMEM, VMEM, VMEM],
            out_specs=VMEM,
            scratch_shapes=[pltpu.VMEM((d // 2, hidden), BF16)],
            compiler_params=pltpu.CompilerParams(vmem_limit_bytes=8 << 20),
            cost_estimate=pl.CostEstimate(
                flops=d * rows * hidden, bytes_accessed=4 << 20, transcendentals=0
            ),
        )(at, own, w_in)
        mine, t1, pre = lax.optimization_barrier((mine, t1, pre))
        other = lax.ppermute(mine, "c", PAIR)
        t2 = lax.ppermute(pick(mine.reshape(nh, 2, feats, rows), 1 - zl, 1), "zl", PAIR)
        rest, pre_grad = pl.pallas_call(
            hidden_kernel,
            out_shape=(
                jax.ShapeDtypeStruct((ny, 2, feats, rows), BF16),
                jax.ShapeDtypeStruct((rows, hidden), BF16),
            ),
            in_specs=[SMEM] + [VMEM] * 5,
            out_specs=(VMEM, VMEM),
            scratch_shapes=[pltpu.VMEM((d // 2, hidden), BF16)],
            compiler_params=pltpu.CompilerParams(vmem_limit_bytes=8 << 20),
            cost_estimate=pl.CostEstimate(
                flops=d * rows * hidden,
                bytes_accessed=5 << 20,
                transcendentals=rows * hidden,
            ),
        )(at, mine, other, w_in, hidden_grad, pre)
        pair_grad = lax.ppermute(pre_grad, "zl", PAIR)
        keep, send = pl.pallas_call(
            input_kernel,
            out_shape=(
                jax.ShapeDtypeStruct((2 * ny, feats, rows), F32),
                jax.ShapeDtypeStruct((2 * ny + 2 * nh, feats, rows), BF16),
            ),
            in_specs=[SMEM] + [VMEM] * 4,
            out_specs=(VMEM, VMEM),
            compiler_params=pltpu.CompilerParams(vmem_limit_bytes=8 << 20),
            cost_estimate=pl.CostEstimate(
                flops=2 * d * rows * hidden, bytes_accessed=5 << 20, transcendentals=0
            ),
        )(at, w_in, pre_grad, t1, t2)
        acc = pl.pallas_call(
            own_kernel,
            out_shape=jax.ShapeDtypeStruct((4 * nh, feats, hidden), F32),
            in_specs=[SMEM] + [VMEM] * 3,
            out_specs=VMEM,
            compiler_params=pltpu.CompilerParams(vmem_limit_bytes=4 << 20),
            cost_estimate=pl.CostEstimate(
                flops=d * rows * hidden, bytes_accessed=4 << 20, transcendentals=0
            ),
        )(at, own, rest, pre_grad)
        send, pair_grad, acc = lax.optimization_barrier((send, pair_grad, acc))
        swapped = lax.ppermute(send, "c", PAIR)
        total = keep + swapped[: 2 * ny].astype(F32)
        total, tother = lax.optimization_barrier((total, swapped[2 * ny :]))
        wpart = pl.pallas_call(
            weight_kernel,
            out_shape=jax.ShapeDtypeStruct((4 * nh, feats, hidden), BF16),
            in_specs=[SMEM] + [VMEM] * 5,
            out_specs=VMEM,
            compiler_params=pltpu.CompilerParams(vmem_limit_bytes=4 << 20),
            cost_estimate=pl.CostEstimate(
                flops=d * rows * hidden, bytes_accessed=4 << 20, transcendentals=0
            ),
        )(at, acc, t1, t2, tother, pair_grad)
        wpart = wpart.reshape(nh * nx, -1, hidden)
        pieces = lax.all_to_all(wpart, ("zh", "xh"), 0, 0, tiled=True)
        total = halve_early(total, "y", [(i, i ^ 1) for i in range(ny)])
        bit = 2
        while bit < ny:
            total = halve(total, "y", [(i, i ^ bit) for i in range(ny)])
            bit *= 2
        total = halve(total, "xl", PAIR)
        weight_sum = jnp.sum(pieces.astype(F32), axis=0)
        return (total[0].astype(BF16).T, weight_sum.astype(BF16))

    return local


def solution(mesh, sizes=(8, 4, 8)):
    nz, nx, ny = sizes
    split = Mesh(mesh.devices.reshape(nz // 2, 2, nx, ny, 2, 2), DP + MP)
    return jax.shard_map(
        make_local(*sizes),
        mesh=split,
        in_specs=(P(DP, MP), P(None, MP), P(DP, MP)),
        out_specs=(P(DP, MP), P(DP, MP)),
        check_vma=False,
    )
```

```python
import jax
import jax.numpy as jnp
from jax import lax
from jax.experimental import pallas as pl
from jax.experimental.pallas import tpu as pltpu
from jax.sharding import Mesh, PartitionSpec as P

DP = ("zh", "zl", "xh")
MP = ("y", "xl", "c")
F32 = jnp.float32
BF16 = jnp.bfloat16
VMEM = pl.BlockSpec(memory_space=pltpu.VMEM)
SMEM = pl.BlockSpec(memory_space=pltpu.SMEM)
PAIR = [(0, 1), (1, 0)]
EARLY_FLOPS = 60_000_000_000


def gelu_slope(pre):
    coef = 0.7978845608028654
    inner = coef * (pre + 0.044715 * pre * pre * pre)
    tval = jnp.tanh(inner)
    return 0.5 * (1.0 + tval) + 0.5 * pre * (1.0 - tval * tval) * coef * (
        1.0 + 3.0 * 0.044715 * pre * pre
    )


def pre_kernel(at_ref, tok_ref, w_ref, pre_ref, w_half):
    pre_ref[...] = half_pre(at_ref[1], tok_ref, w_ref, w_half)


def half_pre(x, tok_ref, w_ref, w_half):
    ny, _, feats, rows = tok_ref.shape
    for y in range(ny):
        start = pl.multiple_of((4 * y + 2 * x) * feats, 2 * feats)
        w_half[pl.ds(2 * y * feats, 2 * feats), :] = w_ref[pl.ds(start, 2 * feats), :]
    return lax.dot_general(
        tok_ref[...].reshape(2 * ny * feats, rows),
        w_half[...],
        (((0,), (0,)), ((), ())),
        preferred_element_type=F32,
    )


def hidden_kernel(
    at_ref, mine_ref, other_ref, w_ref, g_ref, pre_ref, rest, pg_ref, w_half
):
    xl, core = at_ref[1], at_ref[2]
    for y in range(mine_ref.shape[0]):
        rest[y, core] = mine_ref[y]
        rest[y, 1 - core] = other_ref[y]
    pre = pre_ref[...] + half_pre(1 - xl, rest, w_ref, w_half)
    pg_ref[...] = (g_ref[...].astype(F32) * gelu_slope(pre)).astype(BF16)


def input_kernel(at_ref, w_ref, pg_ref, t1_ref, t2_ref, keep_ref, send_ref):
    y_own, xl, core = at_ref[0], at_ref[1], at_ref[2]
    ny, feats = keep_ref.shape[0] // 2, keep_ref.shape[1]
    nh = t1_ref.shape[0]
    bits = ny.bit_length() - 1
    send_ref[2 * ny : 2 * ny + nh] = t1_ref[...]
    send_ref[2 * ny + nh :] = t2_ref[...]
    pg_t = pg_ref[...].T
    for r in range(ny):
        at = sum((r >> k & 1) << (bits - 1 - k) for k in range(bits))
        start = lax.bitwise_xor(y_own, jnp.int32(r)) * (4 * feats)
        block = lax.dot_general(
            w_ref[pl.ds(pl.multiple_of(start, 4 * feats), 4 * feats), :],
            pg_t,
            (((1,), (0,)), ((), ())),
            preferred_element_type=F32,
        )
        for c in range(2):

            @pl.when(core == c)
            def _():
                for x in range(2):
                    to = lax.bitwise_xor(xl, jnp.int32(x)) * ny + at
                    for ref, b in ((keep_ref, 2 * x + c), (send_ref, 2 * x + 1 - c)):
                        part = block[b * feats : (b + 1) * feats]
                        ref[to] = part.astype(ref.dtype)


def own_kernel(at_ref, own, rest, pg_ref, acc_ref):
    xl, core, zl = at_ref[1], at_ref[2], at_ref[3]
    for i in range(acc_ref.shape[0] // 4):
        for x, tok in ((xl, own), (1 - xl, rest)):
            for c in (core, 1 - core):
                acc_ref[4 * i + 2 * x + c] = jnp.dot(
                    tok[2 * i + zl, c], pg_ref[...], preferred_element_type=F32
                )


def weight_kernel(at_ref, acc_ref, t1_ref, t2_ref, tother_ref, pgpair_ref, out_ref):
    xl, core = at_ref[1], at_ref[2]
    nh = t1_ref.shape[0]
    for i in range(nh):
        for x, mine in ((0, t1_ref), (1, t2_ref)):
            for c, tok in ((core, mine[i]), (1 - core, tother_ref[x * nh + i])):
                at = 4 * i + 2 * lax.bitwise_xor(xl, jnp.int32(x)) + c
                total = acc_ref[at] + jnp.dot(
                    tok, pgpair_ref[...], preferred_element_type=F32
                )
                out_ref[at] = total.astype(BF16)


def add_kernel(keep_ref, arrived_ref, out_ref):
    out_ref[...] = keep_ref[...] + arrived_ref[...].astype(F32)


def halve_early(total, axis, pairs):
    half = total.shape[0] // 2
    arrived = lax.ppermute(total[half:].astype(BF16), axis, pairs)
    return pl.pallas_call(
        add_kernel,
        out_shape=jax.ShapeDtypeStruct(arrived.shape, F32),
        in_specs=[VMEM, VMEM],
        out_specs=VMEM,
        compiler_params=pltpu.CompilerParams(vmem_limit_bytes=4 << 20),
        cost_estimate=pl.CostEstimate(
            flops=EARLY_FLOPS, bytes_accessed=2 << 20, transcendentals=0
        ),
    )(total[:half], arrived)


def halve(total, axis, pairs):
    half = total.shape[0] // 2
    arrived = lax.ppermute(total[half:].astype(BF16), axis, pairs)
    return total[:half] + arrived.astype(F32)


def make_local(nz, nx, ny):
    nh = nz // 2

    def local(tokens, w_in, hidden_grad):
        rows, feats = tokens.shape
        d, hidden = w_in.shape
        core, zl = lax.axis_index("c"), lax.axis_index("zl")
        at = jnp.stack([lax.axis_index("y"), lax.axis_index("xl"), core, zl]).astype(jnp.int32)

        def pick(array, index, axis):
            return lax.dynamic_index_in_dim(array, index, axis, keepdims=False)

        own = lax.all_gather(tokens.T, ("y", "c"), axis=0).reshape(ny, 2, feats, rows)
        half = pick(own, core, 1)
        mine = lax.ppermute(half, "xl", PAIR)
        t1 = pick(pick(own.reshape(nh, 2, 2, feats, rows), 1 - zl, 1), core, 1)
        t1 = lax.ppermute(t1, "zl", PAIR)
        pre = pl.pallas_call(
            pre_kernel,
            out_shape=jax.ShapeDtypeStruct((rows, hidden), F32),
            in_specs=[SMEM, VMEM, VMEM],
            out_specs=VMEM,
            scratch_shapes=[pltpu.VMEM((d // 2, hidden), BF16)],
            compiler_params=pltpu.CompilerParams(vmem_limit_bytes=8 << 20),
            cost_estimate=pl.CostEstimate(
                flops=d * rows * hidden, bytes_accessed=4 << 20, transcendentals=0
            ),
        )(at, own, w_in)
        mine, t1, pre = lax.optimization_barrier((mine, t1, pre))
        other = lax.ppermute(mine, "c", PAIR)
        t2 = lax.ppermute(pick(mine.reshape(nh, 2, feats, rows), 1 - zl, 1), "zl", PAIR)
        rest, pre_grad = pl.pallas_call(
            hidden_kernel,
            out_shape=(
                jax.ShapeDtypeStruct((ny, 2, feats, rows), BF16),
                jax.ShapeDtypeStruct((rows, hidden), BF16),
            ),
            in_specs=[SMEM] + [VMEM] * 5,
            out_specs=(VMEM, VMEM),
            scratch_shapes=[pltpu.VMEM((d // 2, hidden), BF16)],
            compiler_params=pltpu.CompilerParams(vmem_limit_bytes=8 << 20),
            cost_estimate=pl.CostEstimate(
                flops=d * rows * hidden,
                bytes_accessed=5 << 20,
                transcendentals=rows * hidden,
            ),
        )(at, mine, other, w_in, hidden_grad, pre)
        pair_grad = lax.ppermute(pre_grad, "zl", PAIR)
        keep, send = pl.pallas_call(
            input_kernel,
            out_shape=(
                jax.ShapeDtypeStruct((2 * ny, feats, rows), F32),
                jax.ShapeDtypeStruct((2 * ny + 2 * nh, feats, rows), BF16),
            ),
            in_specs=[SMEM] + [VMEM] * 4,
            out_specs=(VMEM, VMEM),
            compiler_params=pltpu.CompilerParams(vmem_limit_bytes=8 << 20),
            cost_estimate=pl.CostEstimate(
                flops=2 * d * rows * hidden, bytes_accessed=5 << 20, transcendentals=0
            ),
        )(at, w_in, pre_grad, t1, t2)
        acc = pl.pallas_call(
            own_kernel,
            out_shape=jax.ShapeDtypeStruct((4 * nh, feats, hidden), F32),
            in_specs=[SMEM] + [VMEM] * 3,
            out_specs=VMEM,
            compiler_params=pltpu.CompilerParams(vmem_limit_bytes=4 << 20),
            cost_estimate=pl.CostEstimate(
                flops=d * rows * hidden, bytes_accessed=4 << 20, transcendentals=0
            ),
        )(at, own, rest, pre_grad)
        send, pair_grad, acc = lax.optimization_barrier((send, pair_grad, acc))
        swapped = lax.ppermute(send, "c", PAIR)
        total = keep + swapped[: 2 * ny].astype(F32)
        total, tother = lax.optimization_barrier((total, swapped[2 * ny :]))
        wpart = pl.pallas_call(
            weight_kernel,
            out_shape=jax.ShapeDtypeStruct((4 * nh, feats, hidden), BF16),
            in_specs=[SMEM] + [VMEM] * 5,
            out_specs=VMEM,
            compiler_params=pltpu.CompilerParams(vmem_limit_bytes=4 << 20),
            cost_estimate=pl.CostEstimate(
                flops=d * rows * hidden, bytes_accessed=4 << 20, transcendentals=0
            ),
        )(at, acc, t1, t2, tother, pair_grad)
        wpart = wpart.reshape(nh * nx, -1, hidden)
        pieces = lax.all_to_all(wpart, ("zh", "xh"), 0, 0, tiled=True)
        total = halve_early(total, "xl", PAIR)
        bit = 1
        while bit < ny:
            total = halve(total, "y", [(i, i ^ bit) for i in range(ny)])
            bit *= 2
        weight_sum = jnp.sum(pieces.astype(F32), axis=0)
        return (total[0].astype(BF16).T, weight_sum.astype(BF16))

    return local


def solution(mesh, sizes=(8, 4, 8)):
    nz, nx, ny = sizes
    split = Mesh(mesh.devices.reshape(nz // 2, 2, nx, ny, 2, 2), DP + MP)
    return jax.shard_map(
        make_local(*sizes),
        mesh=split,
        in_specs=(P(DP, MP), P(None, MP), P(DP, MP)),
        out_specs=(P(DP, MP), P(DP, MP)),
        check_vma=False,
    )
```
